32 devices in a mesh: dp: 4 (over y, x), expert: 8 (over z, core).
Axes of the slice: x: 2, y: 2, z: 4, core: 2. Of those that a mesh axis runs over, the one named last changes fastest.
Arguments:
- tokens: bfloat16 [4096, 1024], P(('dp', 'expert')), may hold values from -6 to 6
- expert_id: int32 [4096, 1], P(('dp', 'expert')), may hold values from 0 to 7; in each aligned block of 128 rows (0 to 127, 128 to 255, ...) at most 32 rows name the same one
- gate_prob: bfloat16 [4096], P(('dp', 'expert')), may hold values from 0.29882812 to 1
- w_in: bfloat16 [8, 1024, 4096], P('expert', None, 'dp'), may hold values from -0.1875 to 0.1875
- w_out: bfloat16 [8, 4096, 1024], P('expert', 'dp'), may hold values from -0.09375 to 0.09375
- head: bfloat16 [1024, 512], replicated, may hold values from -0.1875 to 0.1875
- image_cache: bfloat16 [256, 512], P(('dp', 'expert')), may hold values from -25 to 25
- text_cache: bfloat16 [256, 512], P(('dp', 'expert')), may hold values from -5.1 to 5.1
- pair_label: int32 [256], P(('dp', 'expert')), may hold values from 0 to 255, each once
Outputs:
- grad_image: float32 [256, 512], P(('dp', 'expert'))
- grad_in: float32 [8, 1024, 4096], P('expert', None, 'dp')
- grad_out: float32 [8, 4096, 1024], P('expert', 'dp')
The draws below stay inside these ranges and needn't reach their ends.
Inputs may be any that keep to these rules, and one draw needn't show every extreme that they name: `expert_id`: among the 128 tokens of one device no expert is named more than 32 times, a bound that some block reaches. `pair_label`: each caption index appears once.
All inputs are finite; a program needn't handle non-finite values.
Results may differ from the reference program's by a relative error of at most 0.015.
Values may be sent and summed in bfloat16 or wider, within the bound.
A program may use at most 64 MiB of HBM per device.

```python
import math
import jax
import jax.numpy as jnp
import numpy as np
from jax import lax

D = 1024
FF = 4096
E = 512
TOK_DEV = 128
PAIRS_DEV = 8
EXPERTS = 8
CAP = 32
TOKENS = 4096
PAIRS = 256
DEVICES = 32


def base_rows(key):
    return jnp.clip(jax.random.normal(key, (PAIRS, E), jnp.float32), -5.0, 5.0)


def draw_text_cache(key, part):
    base = base_rows(key)
    return base.astype(jnp.bfloat16)


def draw_image_cache(key, part):
    key = jax.random.fold_in(key, 7)
    rows = jnp.clip(jax.random.normal(key, (PAIRS, E), jnp.float32), -5.0, 5.0)
    return rows.astype(jnp.bfloat16)


def levels(key, shape, pieces, least, largest):
    loudness = 1.0
    for position, shards_of in pieces:
        heights = jax.random.uniform(jax.random.fold_in(jax.random.fold_in(key, 6), position), (shards_of,), jnp.float32, least / len(pieces), largest / len(pieces))
        loudness = loudness * jnp.repeat(jnp.exp(heights), shape[position] // shards_of).reshape((-1,) + (1,) * (len(shape) - 1 - position))
    return loudness


def assign_block(own_key, own, number, rows, number_of, top, reach, lean):
    order = jax.random.permutation(own_key, number_of)
    crowded, ordinary = shares(number_of, rows * top, reach, lean, True), shares(number_of, rows * top, reach, lean, False)
    places = jnp.arange(number_of)

    def named(lengths, rotation):
        used = int((lengths > 0).sum())
        fixed = max(1, used // 4)
        passed = fixed + (places - fixed + rotation * (used - fixed)) % max(1, number_of - fixed)
        return jnp.zeros((number_of,), jnp.int32).at[order[jnp.where(places < fixed, places, passed)]].set(jnp.asarray(lengths, jnp.int32))

    lengths = jnp.where(number % 4 == 0, named(crowded, number // 4), named(ordinary, number - number // 4 - 1))
    mixed = jax.random.permutation(jax.random.fold_in(own, 3), number_of)
    giver, sink = mixed[0:number_of // 2 * 2:2], mixed[1:number_of // 2 * 2:2]
    margin = jnp.minimum(lengths[giver] - 1, reach - lengths[sink]) // 2
    margin = jnp.where((giver == order[0]) | (sink == order[0]) | (lengths[sink] == 0), 0, jnp.maximum(margin, 0))
    passed = jax.random.randint(jax.random.fold_in(own, 4), (number_of // 2,), 0, 1 << 20) % (margin + 1)
    lengths = lengths.at[giver].add(-passed).at[sink].add(passed)
    labels = jnp.searchsorted(jnp.cumsum(lengths), jnp.arange(rows * top), side="right").astype(jnp.int32)
    listing = labels.reshape(top, rows).T
    listing = listing[jax.random.permutation(jax.random.fold_in(own, 1), rows)]
    rotation = jax.random.randint(jax.random.fold_in(own, 2), (rows, 1), 0, top)
    return jnp.take_along_axis(listing, (jnp.arange(top)[None, :] + rotation) % top, axis=1)


def shares(count, total, reach, skew, full):
    portions = [(1 << 20) // math.isqrt(rank ** skew) + 1 for rank in range(1, count + 1)]
    largest = reach if full else min(reach, max(-(-total // count), total * portions[0] // sum(portions)))
    least = 1 if total - largest >= count - 1 else 0
    given, surplus = [largest] + [least] * (count - 1), total - largest - least * (count - 1)
    while surplus > 0:
        free = [i for i in range(1, count) if given[i] < largest] or [i for i in range(1, count) if given[i] < reach]
        mass, budget = sum([portions[i] for i in free]), surplus
        for i in free:
            more = min(reach - given[i], max(1, budget * portions[i] // mass), surplus)
            given[i] = given[i] + more
            surplus = surplus - more
    return np.array(given)


def normal_values(stream_key, dims, scale, most, pieces=(), held_as=jnp.bfloat16):
    drawn = jax.random.normal(stream_key, dims, jnp.float32) * scale
    if len(pieces) > 0:
        drawn = levels(stream_key, dims, pieces, -0.22, 0.18) * drawn
    return jnp.clip(drawn, min=-most, max=most).astype(held_as)


def setup_inputs(seed: int = 0) -> dict:
    arg_keys = jax.random.split(jax.random.key(seed), 10)
    tokens = normal_values(arg_keys[0], (TOKENS, D), 1.0, 6.0, ((0, 32),))
    expert_id_keys = jax.random.split(jax.random.fold_in(arg_keys[1], 1), TOKENS // TOK_DEV)
    expert_id_turns = jax.random.permutation(jax.random.fold_in(arg_keys[1], 3), TOKENS // TOK_DEV)
    expert_id = jax.vmap(lambda own, number: assign_block(jax.random.fold_in(arg_keys[1], 2), own, number, TOK_DEV, EXPERTS, 1, CAP, 2))(expert_id_keys, expert_id_turns).reshape((TOKENS, 1))
    gate_prob = jnp.clip(0.29882812 + 0.7011719 * jax.random.uniform(arg_keys[2], (TOKENS,), jnp.float32) ** levels(arg_keys[2], (TOKENS,), ((0, 32),), -0.2, 0.2), 0.29882812, 1.0).astype(jnp.bfloat16)
    w_in = normal_values(arg_keys[3], (EXPERTS, D, FF), D ** -0.5, 0.1875, ((0, 8), (2, 4)))
    w_out = normal_values(arg_keys[4], (EXPERTS, FF, D), FF ** -0.5, 0.09375, ((0, 8), (1, 4)))
    head = normal_values(arg_keys[5], (D, E), D ** -0.5, 0.1875)
    image_cache = draw_image_cache(jax.random.fold_in(arg_keys[9], 71), 0)
    text_cache = draw_text_cache(jax.random.fold_in(arg_keys[9], 71), 0)
    pair_label = jax.random.permutation(arg_keys[8], PAIRS).astype(jnp.int32)
    return {"tokens": tokens, "expert_id": expert_id, "gate_prob": gate_prob, "w_in": w_in, "w_out": w_out, "head": head, "image_cache": image_cache, "text_cache": text_cache, "pair_label": pair_label}


LOGIT_SCALE = 0.125
GELU_K = 0.7978845608
GELU_C = 0.044715


def gelu_parts(pre):
    inner = GELU_K * (pre + GELU_C * pre * pre * pre)
    tangent = jnp.tanh(inner)
    value = 0.5 * pre * (1.0 + tangent)
    slope = 0.5 * (1.0 + tangent) + 0.5 * pre * (1.0 - tangent * tangent) * GELU_K * (1.0 + 3.0 * GELU_C * pre * pre)
    return value, slope


def reference(tokens, expert_id, gate_prob, w_in, w_out, head, image_cache, text_cache, pair_label):
    logits = LOGIT_SCALE * jnp.dot(image_cache, text_cache.T, preferred_element_type=jnp.float32)
    top = jnp.max(logits, axis=1, keepdims=True)
    expo = jnp.exp(logits - top)
    total = jnp.sum(expo, axis=1, keepdims=True)
    weights = expo.astype(jnp.bfloat16)
    mixed = jnp.dot(weights, text_cache, preferred_element_type=jnp.float32) / total
    labelled = text_cache[pair_label].astype(jnp.float32)
    grad_image = LOGIT_SCALE * (mixed - labelled)

    rep_grad = grad_image.reshape(DEVICES, PAIRS_DEV, E)[:, 0, :].astype(jnp.bfloat16)
    cotangent = jnp.dot(rep_grad, head.T, preferred_element_type=jnp.float32).astype(jnp.bfloat16)
    device_of = jnp.arange(TOKENS, dtype=jnp.int32) // TOK_DEV
    out_grad = (gate_prob.astype(jnp.float32)[:, None] * cotangent.astype(jnp.float32)[device_of]).astype(jnp.bfloat16)

    chosen = expert_id[:, 0].astype(jnp.int32)
    onehot = (chosen.reshape(DEVICES, TOK_DEV)[:, :, None] == jnp.arange(EXPERTS, dtype=jnp.int32)[None, None, :]).astype(jnp.float32)
    before = jnp.cumsum(onehot, axis=1) - onehot
    rank = jnp.sum(before * onehot, axis=2).reshape(TOKENS).astype(jnp.int32)
    row = device_of * CAP + rank
    x_buffer = jnp.zeros((EXPERTS, DEVICES * CAP, D), jnp.bfloat16).at[chosen, row].set(tokens)
    g_buffer = jnp.zeros((EXPERTS, DEVICES * CAP, D), jnp.bfloat16).at[chosen, row].set(out_grad)

    def one_expert(packed):
        x_rows, dy_rows, first, second = packed
        pre = jnp.dot(x_rows, first, preferred_element_type=jnp.float32)
        value, slope = gelu_parts(pre)
        hidden = value.astype(jnp.bfloat16)
        back = jnp.dot(dy_rows, second.T, preferred_element_type=jnp.float32)
        hidden_grad = (back * slope).astype(jnp.bfloat16)
        grad_first = jnp.dot(x_rows.T, hidden_grad, preferred_element_type=jnp.float32)
        grad_second = jnp.dot(hidden.T, dy_rows, preferred_element_type=jnp.float32)
        return grad_first, grad_second

    grad_in, grad_out = lax.map(one_expert, (x_buffer, g_buffer, w_in, w_out))
    return grad_image, grad_in, grad_out
```

```python
import jax
import jax.numpy as jnp
from jax import lax
from jax.sharding import PartitionSpec as P

LOGIT_SCALE = 0.125
GELU_K = 0.7978845608
GELU_C = 0.044715


def gelu_parts(pre):
    inner = GELU_K * (pre + GELU_C * pre * pre * pre)
    tangent = jnp.tanh(inner)
    value = 0.5 * pre * (1.0 + tangent)
    slope = 0.5 * (1.0 + tangent) + 0.5 * pre * (1.0 - tangent * tangent) * GELU_K * (
        1.0 + 3.0 * GELU_C * pre * pre
    )
    return (value, slope)


def expert_terms(x_rows, gates, cots, first, second, capacity):
    n_img = cots.shape[0]
    pre = jnp.dot(x_rows, first, preferred_element_type=jnp.float32)
    value, slope = gelu_parts(pre)
    hidden = value.astype(jnp.bfloat16).astype(jnp.float32)
    back = lax.dot_general(
        cots, second, (((1,), (1,)), ((), ())), preferred_element_type=jnp.float32
    )
    units = back.shape[1]
    gated = gates.astype(jnp.float32).reshape(n_img, capacity, 1)
    hidden_grad = (gated * back[:, None, :] * slope.reshape(n_img, capacity, units)).astype(jnp.bfloat16)
    grad_first = lax.dot_general(
        x_rows, hidden_grad.reshape(-1, units), (((0,), (0,)), ((), ())), preferred_element_type=jnp.float32
    )
    summed = jnp.sum(gated * hidden.reshape(n_img, capacity, units), axis=1).astype(jnp.bfloat16)
    grad_second = lax.dot_general(
        summed, cots, (((0,), (0,)), ((), ())), preferred_element_type=jnp.float32
    )
    return (grad_first, grad_second)


def caption_block(carry, image_cache, pair_label, piece):
    run_top, run_total, run_mix, run_label = carry
    logits = LOGIT_SCALE * lax.dot_general(
        image_cache, piece, (((1,), (1,)), ((), ())), preferred_element_type=jnp.float32
    )
    new_top = jnp.maximum(run_top, jnp.max(logits, axis=1, keepdims=True))
    expo = jnp.exp(logits - new_top)
    new_total = jnp.sum(expo, axis=1, keepdims=True)
    new_mix = jnp.dot(expo.astype(jnp.bfloat16), piece, preferred_element_type=jnp.float32)
    columns = jnp.arange(piece.shape[0], dtype=jnp.int32)
    hits = (pair_label[:, None] == columns[None, :]).astype(jnp.bfloat16)
    new_label = jnp.dot(hits, piece, preferred_element_type=jnp.float32)
    return (new_top, new_total, new_mix, new_label)


def body(tokens, expert_id, gate_prob, w_in, w_out, head, image_cache, text_cache, pair_label):
    n_tok = tokens.shape[0]
    n_exp = lax.axis_size("expert")
    capacity = 2 * n_tok // n_exp
    n_pairs = image_cache.shape[0]
    width = image_cache.shape[1]
    start_carry = (
        jnp.full((n_pairs, 1), -1e30, jnp.float32),
        jnp.zeros((n_pairs, 1), jnp.float32),
        jnp.zeros((n_pairs, width), jnp.float32),
        jnp.zeros((n_pairs, width), jnp.float32),
    )
    captions = lax.all_gather(text_cache, ("dp", "expert"), axis=0, tiled=True)
    result = caption_block(start_carry, image_cache, pair_label, captions)
    grad_image = LOGIT_SCALE * (result[2] / result[1] - result[3])
    rep_grad = grad_image[0].astype(jnp.bfloat16)
    cotangent = jnp.dot(head, rep_grad, preferred_element_type=jnp.float32).astype(jnp.bfloat16)
    chosen = expert_id[:, 0]
    onehot = (chosen[:, None] == jnp.arange(n_exp, dtype=jnp.int32)[None, :]).astype(jnp.float32)
    lower = (jnp.arange(n_tok)[:, None] > jnp.arange(n_tok)[None, :]).astype(jnp.float32)
    before = jnp.dot(lower, onehot, precision=lax.Precision.HIGHEST)
    rank = jnp.sum(before * onehot, axis=1).astype(jnp.int32)
    position = chosen * capacity + rank
    dispatch = (position[:, None] == jnp.arange(n_exp * capacity, dtype=jnp.int32)[None, :]).astype(
        jnp.bfloat16
    )
    width_in = tokens.shape[1]
    carried = jnp.concatenate(
        [tokens, jnp.broadcast_to(gate_prob[:, None], (n_tok, 128))], axis=1
    )
    x_buffer = lax.dot_general(
        dispatch, carried, (((0,), (0,)), ((), ())), preferred_element_type=jnp.float32
    ).astype(jnp.bfloat16)
    x_recv = lax.all_to_all(x_buffer, "expert", split_axis=0, concat_axis=0, tiled=True)
    rows = lax.all_gather(x_recv, "dp", axis=0, tiled=True)
    cots = lax.all_gather(cotangent[None], ("dp", "expert"), axis=0, tiled=True)
    grads = expert_terms(
        rows[:, :width_in], rows[:, width_in], cots, w_in[0], w_out[0], capacity
    )
    return (grad_image, grads[0][None], grads[1][None])


def solution(mesh):
    placed = (
        P(("dp", "expert"), None),
        P(("dp", "expert"), None),
        P(("dp", "expert")),
        P("expert", None, "dp"),
        P("expert", "dp", None),
        P(),
        P(("dp", "expert"), None),
        P(("dp", "expert"), None),
        P(("dp", "expert")),
    )
    return jax.shard_map(
        body,
        mesh=mesh,
        in_specs=placed,
        out_specs=(P(("dp", "expert"), None), P("expert", None, "dp"), P("expert", "dp", None)),
        check_vma=False,
    )
```

```python
import functools

import jax
import jax.numpy as jnp
from jax import lax
from jax.experimental import pallas as pl
from jax.experimental.pallas import tpu as pltpu
from jax.sharding import PartitionSpec as P

LOGIT_SCALE = 0.125
GELU_K = 0.7978845608
GELU_C = 0.044715
LANES = 128
BF = jnp.bfloat16
F32 = jnp.float32


def gelu_parts(pre):
    inner = GELU_K * (pre + GELU_C * pre * pre * pre)
    tangent = jnp.tanh(inner)
    value = 0.5 * pre * (1.0 + tangent)
    slope = 0.5 * (1.0 + tangent) + 0.5 * pre * (1.0 - tangent * tangent) * GELU_K * (
        1.0 + 3.0 * GELU_C * pre * pre
    )
    return (value, slope)


def dot_t(a, b):
    return lax.dot_general(a, b, (((1,), (1,)), ((), ())), preferred_element_type=F32)


def kernel(
    n_dp, n_exp, capacity,
    tokens_ref, id_ref, gate_ref, image_ref, text_ref, label_ref, head_hbm, w_in_hbm, w_out_hbm,
    grad_image_ref, x_ref, hg_ref, sum_ref, cots_ref,
    head_ref, w_in_ref, w_out_ref, xbuf, xall, tall, call, back_ref, sums,
    load_sem, x1_send, x1_recv, x2_send, x2_recv, t1_send, t1_recv, t2_send, t2_recv,
    c1_send, c1_recv, c2_send, c2_recv,
):
    dp = lax.axis_index("dp")
    ex = lax.axis_index("expert")
    n_tok, width = tokens_ref.shape
    wide = xbuf.shape[2]
    slots = n_exp * capacity
    units = w_in_ref.shape[1]

    loads = [
        pltpu.make_async_copy(src, dst, load_sem.at[i])
        for i, (src, dst) in enumerate(
            ((head_hbm, head_ref), (w_in_hbm, w_in_ref), (w_out_hbm, w_out_ref))
        )
    ]
    for load in loads:
        load.start()

    def ex_at(k):
        return lax.rem(ex + k, n_exp)

    def ex_from(k):
        return lax.rem(ex + n_exp - k, n_exp)

    def dp_at(k):
        return lax.rem(dp + k, n_dp)

    def dp_from(k):
        return lax.rem(dp + n_dp - k, n_dp)

    def loop(lo, hi, fn):
        def step(k, c):
            fn(k)
            return c

        lax.fori_loop(lo, hi, step, 0)

    def over_ex(src, dst, send, recv, peer):
        return pltpu.make_async_remote_copy(
            src_ref=src, dst_ref=dst, send_sem=send, recv_sem=recv,
            device_id={"expert": peer}, device_id_type=pl.DeviceIdType.MESH,
        )

    def over_dp(src, dst, send, recv, peer):
        return pltpu.make_async_remote_copy(
            src_ref=src, dst_ref=dst, send_sem=send, recv_sem=recv,
            device_id={"dp": peer}, device_id_type=pl.DeviceIdType.MESH,
        )

    def t1(k, who):
        return over_ex(tall.at[dp, who], tall.at[dp, who], t1_send.at[k], t1_recv.at[who], ex_at(k))

    def c1(k, who):
        return over_ex(call.at[dp, who], call.at[dp, who], c1_send.at[k], c1_recv.at[who], ex_at(k))

    def x1(k, block, who):
        return over_ex(xbuf.at[block], xall.at[dp, who], x1_send.at[k], x1_recv.at[who], ex_at(k))

    def t2(k, row):
        return over_dp(tall.at[row], tall.at[row], t2_send.at[k], t2_recv.at[row], dp_at(k))

    def c2(k, row):
        return over_dp(call.at[row], call.at[row], c2_send.at[k], c2_recv.at[row], dp_at(k))

    def x2(k, row, j):
        return over_dp(
            xall.at[row, j], xall.at[row, j], x2_send.at[k, j], x2_recv.at[row, j], dp_at(k)
        )

    barrier = pltpu.get_barrier_semaphore()
    loop(1, n_exp, lambda k: pl.semaphore_signal(
        barrier, inc=1, device_id={"expert": ex_at(k)}, device_id_type=pl.DeviceIdType.MESH))
    loop(1, n_dp, lambda k: pl.semaphore_signal(
        barrier, inc=1, device_id={"dp": dp_at(k)}, device_id_type=pl.DeviceIdType.MESH))

    half = text_ref.shape[1] // 2
    text = text_ref[...].astype(F32)
    tall[dp, ex] = jnp.concatenate([text[:, :half], text[:, half:]], axis=0).astype(BF)

    own = jnp.broadcast_to(id_ref[...].astype(F32), (n_tok, n_tok))
    other = own.T
    earlier = lax.broadcasted_iota(jnp.int32, (n_tok, n_tok), 0) < lax.broadcasted_iota(
        jnp.int32, (n_tok, n_tok), 1
    )
    rank = jnp.sum(jnp.where((own == other) & earlier, 1.0, 0.0), axis=0, keepdims=True)
    position = (other[:1] * capacity + rank).astype(jnp.int32)
    dispatch = jnp.where(
        lax.broadcasted_iota(jnp.int32, (slots, n_tok), 0) == position, 1.0, 0.0
    ).astype(BF)
    gate = jnp.broadcast_to(gate_ref[...].astype(F32), (n_tok, n_tok)).T.astype(BF)
    x_slots = jnp.dot(dispatch, tokens_ref[...], preferred_element_type=F32)
    g_slots = jnp.dot(dispatch, gate, preferred_element_type=F32)
    xbuf[:, :, :width] = x_slots.reshape(n_exp, capacity, width).astype(BF)
    xbuf[:, :, width:] = g_slots.reshape(n_exp, capacity, wide - width).astype(BF)

    pl.semaphore_wait(barrier, n_exp - 1 + n_dp - 1)

    loop(1, n_exp, lambda k: t1(k, ex).start())
    loop(1, n_exp, lambda k: x1(k, ex_at(k), ex).start())
    xall[dp, ex] = xbuf[ex]
    loop(1, n_dp, lambda k: x2(k, dp, ex).start())

    loop(1, n_exp, lambda k: t1(k, ex_from(k)).wait_recv())
    loop(1, n_dp, lambda k: t2(k, dp).start())

    def forward(k):
        j = ex_from(k)
        x1(k, ex, j).wait_recv()
        loop(1, n_dp, lambda m: x2(m, dp, j).start())

    middle = n_exp // 2
    loop(1, middle, forward)

    loop(1, n_dp, lambda k: t2(k, dp_from(k)).wait_recv())
    n_img = n_dp * n_exp
    pairs = text_ref.shape[0]
    every = tall[...].astype(F32).reshape(n_img, 2 * pairs, half)
    captions = jnp.concatenate(
        [every[:, :pairs].reshape(n_img * pairs, half), every[:, pairs:].reshape(n_img * pairs, half)],
        axis=1,
    ).astype(BF)
    logits = LOGIT_SCALE * dot_t(image_ref[...], captions)
    expo = jnp.exp(logits - jnp.max(logits, axis=1, keepdims=True))
    total = jnp.sum(expo, axis=1, keepdims=True)
    mixed = jnp.dot(expo.astype(BF), captions, preferred_element_type=F32) / total
    columns = lax.broadcasted_iota(jnp.int32, logits.shape, 1)
    hits = jnp.where(label_ref[...] == columns, 1.0, 0.0).astype(BF)
    grad_image = LOGIT_SCALE * (mixed - jnp.dot(hits, captions, preferred_element_type=F32))
    grad_image_ref[...] = grad_image
    loads[0].wait()
    cotangent = dot_t(grad_image.astype(BF), head_ref[...]).astype(BF).astype(F32)
    for k in range(width // LANES):
        call[dp, ex, k : k + 1, :] = cotangent[:1, k * LANES : (k + 1) * LANES]
    loop(1, n_exp, lambda k: c1(k, ex).start())

    loop(middle, n_exp, forward)

    loop(1, n_exp, lambda k: c1(k, ex_from(k)).wait_recv())
    loop(1, n_dp, lambda k: c2(k, dp).start())
    loads[1].wait()
    loads[2].wait()
    loop(1, n_dp, lambda k: c2(k, dp_from(k)).wait_recv())
    cots = jnp.concatenate(
        [call[:, :, k, :].reshape(n_img, LANES) for k in range(width // LANES)], axis=1
    ).astype(BF)
    cots_ref[...] = cots
    back = dot_t(cots, w_out_ref[...])
    back_ref[...] = back.reshape(n_dp, n_exp, units)

    tile = min(256, units)

    def expert_rows(row):
        block = xall[row]
        if capacity % 16:
            block = block.astype(F32).reshape(slots, wide).astype(BF)
        else:
            block = block.reshape(slots, wide)
        rows = block[:, :width]
        gates = block[:, width : width + LANES].astype(F32)
        gates = jnp.concatenate([gates] * (tile // LANES), axis=1)
        at = pl.ds(pl.multiple_of(row * slots, slots), slots)
        x_ref[at, :] = rows
        for c in range(units // tile):
            cols = slice(c * tile, (c + 1) * tile)
            pre = jnp.dot(rows, w_in_ref[:, cols], preferred_element_type=F32)
            value, slope = gelu_parts(pre)
            hidden = value.astype(BF).astype(F32) * gates
            slope = (slope * gates).reshape(n_exp, capacity, tile)
            hg = slope * back_ref[row, :, cols][:, None, :]
            hg_ref[at, cols] = hg.reshape(slots, tile).astype(BF)
            sums[row, :, cols] = jnp.sum(hidden.reshape(n_exp, capacity, tile), axis=1)

    def remote_rows(k):
        row = dp_from(k)
        loop(0, n_exp, lambda j: x2(k, row, j).wait_recv())
        expert_rows(row)

    expert_rows(dp)
    loop(1, n_dp, remote_rows)
    sum_ref[...] = sums[...].reshape(n_img, units).astype(BF)

    def finish_ex(k):
        t1(k, ex).wait_send()
        c1(k, ex).wait_send()
        x1(k, ex_at(k), ex).wait_send()

    def finish_dp(k):
        t2(k, dp).wait_send()
        c2(k, dp).wait_send()
        loop(0, n_exp, lambda j: x2(k, dp, j).wait_send())

    loop(1, n_exp, finish_ex)
    loop(1, n_dp, finish_dp)


def body(tokens, expert_id, gate_prob, w_in, w_out, head, image_cache, text_cache, pair_label):
    n_tok, width = tokens.shape
    n_exp = lax.axis_size("expert")
    n_dp = lax.axis_size("dp")
    capacity = 2 * n_tok // n_exp
    slots = n_exp * capacity
    n_img = n_dp * n_exp
    units = w_in.shape[2]
    pairs, emb = text_cache.shape
    wide = width + LANES
    vmem = pl.BlockSpec(memory_space=pltpu.VMEM)
    hbm = pl.BlockSpec(memory_space=pl.ANY)
    dma = pltpu.SemaphoreType.DMA
    grad_image, rows, hidden_grad, summed, cots = pl.pallas_call(
        functools.partial(kernel, n_dp, n_exp, capacity),
        out_shape=(
            jax.ShapeDtypeStruct((pairs, emb), F32),
            jax.ShapeDtypeStruct((n_dp * slots, width), BF),
            jax.ShapeDtypeStruct((n_dp * slots, units), BF),
            jax.ShapeDtypeStruct((n_img, units), BF),
            jax.ShapeDtypeStruct((n_img, width), BF),
        ),
        in_specs=[vmem] * 6 + [hbm] * 3,
        out_specs=(vmem,) * 5,
        scratch_shapes=[
            pltpu.VMEM(head.shape, BF),
            pltpu.VMEM((width, units), BF),
            pltpu.VMEM((units, width), BF),
            pltpu.VMEM((n_exp, capacity, wide), BF),
            pltpu.VMEM((n_dp, n_exp, capacity, wide), BF),
            pltpu.VMEM((n_dp, n_exp, 2 * pairs, emb // 2), BF),
            pltpu.VMEM((n_dp, n_exp, width // LANES, LANES), F32),
            pltpu.VMEM((n_dp, n_exp, units), F32),
            pltpu.VMEM((n_dp, n_exp, units), F32),
            dma((3,)),
            dma((n_exp,)), dma((n_exp,)), dma((n_dp, n_exp)), dma((n_dp, n_exp)),
            dma((n_exp,)), dma((n_exp,)), dma((n_dp,)), dma((n_dp,)),
            dma((n_exp,)), dma((n_exp,)), dma((n_dp,)), dma((n_dp,)),
        ],
        compiler_params=pltpu.CompilerParams(
            collective_id=0, has_side_effects=True, vmem_limit_bytes=56 * 2**20
        ),
    )(
        tokens, expert_id, gate_prob.reshape(1, n_tok), image_cache, text_cache,
        pair_label.reshape(pairs, 1), head, w_in[0], w_out[0],
    )
    grad_first = lax.dot_general(
        rows, hidden_grad, (((0,), (0,)), ((), ())), preferred_element_type=F32
    )
    grad_second = lax.dot_general(
        summed, cots, (((0,), (0,)), ((), ())), preferred_element_type=F32
    )
    return (grad_image, grad_first[None], grad_second[None])


def solution(mesh):
    placed = (
        P(("dp", "expert"), None),
        P(("dp", "expert"), None),
        P(("dp", "expert")),
        P("expert", None, "dp"),
        P("expert", "dp", None),
        P(),
        P(("dp", "expert"), None),
        P(("dp", "expert"), None),
        P(("dp", "expert")),
    )
    return jax.shard_map(
        body,
        mesh=mesh,
        in_specs=placed,
        out_specs=(P(("dp", "expert"), None), P("expert", None, "dp"), P("expert", "dp", None)),
        check_vma=False,
    )
```
